256 devices in a mesh: grp: 8 (over z_lo, y), loc: 32 (over z_hi, x, core).
Axes of the slice: x: 4, y: 4, z: 8 (z_hi: 4, z_lo: 2; z = z_hi * 2 + z_lo), core: 2. Of those that a mesh axis runs over, the one named last changes fastest.
Arguments:
- hidden_states: bfloat16 [131072, 4096], P(('grp', 'loc')), may hold values from -50 to 50
- norm_gain: float32 [4096], replicated, may hold values from 0.1 to 1.9
- master_weight: float32 [4096, 512], P(('grp', 'loc')), may hold values from -0.09375 to 0.09375
- first_moment: float32 [4096, 512], P(('grp', 'loc')), may hold values from -1.5 to 1.5
- second_moment: float32 [4096, 512], P(('grp', 'loc')), may hold values from 0.01 to 1
- token_ids: int32 [131072], P(('grp', 'loc')), may hold values from 0 to 128255
- out_cotangent: bfloat16 [131072, 512], P(('grp', 'loc')), may hold values from -6 to 6
Outputs:
- value_heads: bfloat16 [131072, 512], P(('grp', 'loc'))
- input_grad: bfloat16 [131072, 4096], P(('grp', 'loc'))
- gain_grad: float32 [4096], replicated
- new_master: float32 [4096, 512], P(('grp', 'loc'))
- new_first: float32 [4096, 512], P(('grp', 'loc'))
- new_second: float32 [4096, 512], P(('grp', 'loc'))
The draws below stay inside these ranges and needn't reach their ends.
All inputs are finite; a program needn't handle non-finite values.
Results may differ from the reference program's by a relative error of at most 0.0057.
Values may be sent and summed in bfloat16 or wider, within the bound.
No kernel may reach another device: no remote copies, remote signals or barrier semaphores. Data moves between devices by JAX's collectives and lax.ppermute only.
A program may use at most 128 MiB of HBM per device.

```python
import math
import jax
import jax.numpy as jnp
from jax import lax

DW = 4096
HV = 512
VOCAB = 128256
RESERVED = 256
STEP = 10
TOK_DEV = 512
TOKENS = 131072


def draw_hidden_states(key, part):
    key = jax.random.fold_in(key, 7)
    base_key, row_key, column_key = jax.random.split(key, 3)
    base = jnp.clip(jax.random.normal(base_key, (TOKENS, DW), jnp.float32), -4.0, 4.0)
    row_scale = jnp.exp(jax.random.uniform(row_key, (TOKENS, 1), jnp.float32, 0.0, math.log(10.0)))
    column_scale = jnp.exp(jax.random.uniform(column_key, (1, DW), jnp.float32, 0.0, math.log(10.0)))
    return (0.125 * base * row_scale * column_scale).astype(jnp.bfloat16)


def touch_ends(drawn, key, least, top_value):
    longest = drawn.shape.index(max(drawn.shape))
    spots = []
    for shift in (0, 1):
        where = [jax.random.randint(jax.random.fold_in(key, axis), (), 0, length) for axis, length in enumerate(drawn.shape)]
        where[longest] = (where[longest] + shift) % drawn.shape[longest]
        spots.append(tuple(where))
    return drawn.at[spots[0]].set(least).at[spots[1]].set(top_value)


def steps_of(stream_key, extent, cuts, low, largest):
    level = 1.0
    for dim, shards_of in cuts:
        draws = jax.random.uniform(jax.random.fold_in(jax.random.fold_in(stream_key, 6), dim), (shards_of,), jnp.float32, low / len(cuts), largest / len(cuts))
        level = level * jnp.repeat(jnp.exp(draws), extent[dim] // shards_of).reshape((-1,) + (1,) * (len(extent) - 1 - dim))
    return level


def bell_draw(stream_key, extent, spread, limit, cuts=(), held_as=jnp.bfloat16):
    result = spread * jax.random.normal(stream_key, extent, jnp.float32)
    if cuts:
        result = result * steps_of(stream_key, extent, cuts, -0.22, 0.18)
    return jnp.clip(result, -limit, limit).astype(held_as)


def setup_inputs(seed: int = 0) -> dict:
    seeds = jax.random.split(jax.random.key(seed), 8)
    hidden_states = draw_hidden_states(jax.random.fold_in(seeds[7], 71), 0)
    norm_gain = jnp.clip(1.0 + 0.18 * jax.random.normal(seeds[1], (DW,), jnp.float32), 0.1, 1.9)
    master_weight = bell_draw(seeds[2], (DW, HV), DW ** -0.5, 0.09375, ((0, 256),), jnp.float32)
    first_moment = bell_draw(seeds[3], (DW, HV), 0.1, 1.5, ((0, 256),), jnp.float32)
    second_moment = jnp.clip(jnp.exp(math.log(1.0) - 4.6051702 * jax.random.uniform(seeds[4], (DW, HV), jnp.float32) ** steps_of(seeds[4], (DW, HV), ((0, 256),), -0.2, 0.2)), 0.01, 1.0)
    token_ids = touch_ends(jax.random.randint(seeds[5], (TOKENS,), 0, VOCAB), jax.random.fold_in(seeds[5], 1), 0, VOCAB - 1).astype(jnp.int32)
    out_cotangent = bell_draw(seeds[6], (TOKENS, HV), 1.0, 6.0, ((0, 256),))
    return dict(hidden_states=hidden_states, norm_gain=norm_gain, master_weight=master_weight, first_moment=first_moment, second_moment=second_moment, token_ids=token_ids, out_cotangent=out_cotangent)


norm_epsilon = 1e-05
beta_one = 0.9
beta_two = 0.95
adam_epsilon = 1e-08
learning_rate = 0.001
weight_decay = 0.1

def reference(hidden_states, norm_gain, master_weight, first_moment, second_moment, token_ids, out_cotangent):
    weight_bf = master_weight.astype(jnp.bfloat16)
    blocks = TOKENS // TOK_DEV
    states_all = hidden_states.reshape(blocks, TOK_DEV, DW)
    cot_all = out_cotangent.reshape(blocks, TOK_DEV, HV)
    ids_all = token_ids.reshape(blocks, TOK_DEV)

    def step_block(carry, inputs):
        grad_sum, gain_sum = carry
        block_states, block_cot, block_ids = inputs
        states = block_states.astype(jnp.float32)
        inverse_rms = lax.rsqrt(lax.optimization_barrier(jnp.mean(states * states, axis=1, keepdims=True)) + norm_epsilon)
        scaled = states * inverse_rms
        normed = (scaled * norm_gain).astype(jnp.bfloat16)
        values = jnp.dot(normed, weight_bf, preferred_element_type=jnp.float32).astype(jnp.bfloat16)
        masked = jnp.where((block_ids >= RESERVED)[:, None], block_cot, jnp.zeros_like(block_cot))
        grad_sum = grad_sum + lax.dot_general(normed, masked, (((0,), (0,)), ((), ())), preferred_element_type=jnp.float32)
        back_grad = lax.dot_general(masked, weight_bf, (((1,), (1,)), ((), ())), preferred_element_type=jnp.float32)
        weighted = back_grad * norm_gain
        inner = lax.optimization_barrier(jnp.mean(weighted * scaled, axis=1, keepdims=True))
        input_grad = ((weighted - scaled * inner) * inverse_rms).astype(jnp.bfloat16)
        gain_sum = gain_sum + lax.optimization_barrier(jnp.sum(back_grad * scaled, axis=0))
        return ((grad_sum, gain_sum), (values, input_grad))
    start_carry = (jnp.zeros((DW, HV), jnp.float32), jnp.zeros((DW,), jnp.float32))
    (grad_sum, gain_sum), (values, grads) = lax.scan(step_block, start_carry, (states_all, cot_all, ids_all))
    grad_scale = 1.0 / math.sqrt(TOKENS)
    weight_grad = grad_sum * grad_scale
    gain_grad = gain_sum * grad_scale
    new_first = beta_one * first_moment + (1.0 - beta_one) * weight_grad
    new_second = beta_two * second_moment + (1.0 - beta_two) * weight_grad * weight_grad
    first_bias = 1.0 - beta_one ** STEP
    second_bias = 1.0 - beta_two ** STEP
    update = new_first / first_bias / (jnp.sqrt(new_second / second_bias) + adam_epsilon)
    new_master = master_weight - learning_rate * (update + weight_decay * master_weight)
    value_heads = values.reshape(TOKENS, HV)
    input_grad = grads.reshape(TOKENS, DW)
    return (value_heads, input_grad, gain_grad, new_master, new_first, new_second)
```

```python
import math

import jax
import jax.numpy as jnp
import numpy as np
from jax import lax
from jax.experimental import pallas as pl
from jax.experimental.pallas import tpu as pltpu
from jax.sharding import PartitionSpec as P

RESERVED = 256
STEP = 10

norm_epsilon = 1e-05
beta_one = 0.9
beta_two = 0.95
adam_epsilon = 1e-08
learning_rate = 0.001
weight_decay = 0.1

bf16 = jnp.bfloat16
f32 = jnp.float32
AXES = ("grp", "loc")
DEVICES = 256

CORE = 1
X1, X3, Y1, Y3 = 2, 6, 32, 96
Z1, Z3, Z7 = 128, 136, 152
STEPS = (CORE, (X1, Y1), (X3, Y3), (Y1, X1), (Y3, X3), Z7, Z3, Z1)


def mask_of(mask, core):
    return mask[core] if isinstance(mask, tuple) else mask


def offsets(core):
    half = len(STEPS) - 1
    own, other = ([0], [0])
    for mask in STEPS[:0:-1]:
        own = own + [o ^ mask_of(mask, core) for o in own]
        other = other + [o ^ mask_of(mask, 1 - core) for o in other]
    return own + [o ^ CORE for o in other]


OFFSET_OF = np.array([offsets(0), offsets(1)], np.int32)
POSITION_OF = np.argsort(OFFSET_OF, axis=1).astype(np.int32)


def exchange(x, mask):
    pairs = [(i, i ^ mask_of(mask, i & 1)) for i in range(DEVICES)]
    return lax.ppermute(x, AXES, pairs)


def column(row):
    return jnp.transpose(jnp.broadcast_to(row, (8, row.shape[1])))[:, :1]


def grad_kernel(me_ref, pos_ref, h_ref, gain_ref, cot_ref, ids_ref, inv_ref, keep_ref, send_ref, blk_ref):
    tokens, features = h_ref.shape
    width = 512
    total = jnp.zeros((tokens, 128), f32)
    for j in range(features // 128):
        x = h_ref[:, 128 * j : 128 * j + 128].astype(f32)
        total = total + x * x
    mean = jnp.sum(total, axis=1, keepdims=True) * (1.0 / features)
    inv = lax.rsqrt(mean + norm_epsilon)
    inv_ref[...] = inv
    live = column(ids_ref[...]) >= RESERVED
    masked = jnp.where(live, cot_ref[...], jnp.zeros_like(cot_ref))
    me = me_ref[0]
    core = jnp.bitwise_and(me, 1)

    def block(j, carry):
        at = pl.ds(pl.multiple_of(j * width, width), width)
        normed = ((h_ref[:, at].astype(f32) * inv) * gain_ref[:, at]).astype(bf16)
        part = lax.dot_general(normed, masked, (((0,), (0,)), ((), ())), preferred_element_type=f32)
        blk_ref[...] = part.reshape(blk_ref.shape)
        for i in range(width // 32):
            own = 2 * i + core
            away = 2 * i + (1 - core)
            p = pos_ref[core, jnp.bitwise_xor(j * (width // 16) + own, me)]
            q = pos_ref[core, jnp.bitwise_xor(j * (width // 16) + away, me)] - DEVICES // 2
            keep_ref[p] = blk_ref[own]
            send_ref[q] = blk_ref[away].astype(bf16)
        return carry

    lax.fori_loop(0, features // width, block, 0)


def local_grad(me, hidden, gain, cot, ids):
    tokens, features = hidden.shape
    outs = cot.shape[1]
    half = features // 32
    vmem = pl.BlockSpec(memory_space=pltpu.VMEM)
    smem = pl.BlockSpec(memory_space=pltpu.SMEM)
    return pl.pallas_call(
        grad_kernel,
        out_shape=(
            jax.ShapeDtypeStruct((tokens, 1), f32),
            jax.ShapeDtypeStruct((half, 16, outs), f32),
            jax.ShapeDtypeStruct((half, 16, outs), bf16),
        ),
        in_specs=[smem, smem, vmem, vmem, vmem, vmem],
        out_specs=(vmem, vmem, vmem),
        scratch_shapes=[pltpu.VMEM((32, 16, outs), f32)],
        compiler_params=pltpu.CompilerParams(vmem_limit_bytes=48 * 2**20),
        cost_estimate=pl.CostEstimate(
            flops=2 * tokens * features * outs, bytes_accessed=12 * 2**20, transcendentals=0
        ),
        name="local_grad",
    )(me, jnp.asarray(POSITION_OF), hidden, gain, cot, ids)


def both_kernel(me_ref, off_ref, h_ref, inv_ref, gain_ref, cot_ref, ids_ref, own_ref, other_ref, values_ref, grad_ref, w_ref, wt_ref):
    tokens, features = h_ref.shape
    width = 512
    me = me_ref[0]
    core = jnp.bitwise_and(me, 1)
    half = DEVICES // 2

    @pl.when(pl.program_id(0) == 0)
    def _():
        def place(p, carry):
            w_ref[jnp.bitwise_xor(off_ref[core, p], me)] = own_ref[p]
            w_ref[jnp.bitwise_xor(off_ref[core, p + half], me)] = other_ref[p]
            return carry

        lax.fori_loop(0, half, place, 0, unroll=8)

    inv = inv_ref[...]
    live = column(ids_ref[...]) >= RESERVED
    masked = jnp.where(live, cot_ref[...], jnp.zeros_like(cot_ref))
    values = jnp.zeros(values_ref.shape, f32)
    inner = jnp.zeros((tokens, 128), f32)
    for j in range(features // width):
        at = slice(j * width, j * width + width)
        w = w_ref[j * (width // 16) : (j + 1) * (width // 16)].reshape(width, w_ref.shape[2])
        gain = gain_ref[:, at]
        scaled = h_ref[:, at].astype(f32) * inv
        values = values + jnp.dot((scaled * gain).astype(bf16), w, preferred_element_type=f32)
        back = lax.dot_general(masked, w, (((1,), (1,)), ((), ())), preferred_element_type=f32)
        weighted = back * gain
        wt_ref[:, at] = weighted
        prod = weighted * scaled
        for k in range(width // 128):
            inner = inner + prod[:, 128 * k : 128 * k + 128]
    values_ref[...] = values.astype(bf16)
    mean = jnp.sum(inner, axis=1, keepdims=True) * (1.0 / features)
    for j in range(features // width):
        at = slice(j * width, j * width + width)
        scaled = h_ref[:, at].astype(f32) * inv
        grad_ref[:, at] = ((wt_ref[:, at] - scaled * mean) * inv).astype(bf16)


def values_and_input_grad(me, hidden, inv, gain, cot, ids, own, other):
    tokens, features = hidden.shape
    outs = cot.shape[1]
    rows = 256
    smem = pl.BlockSpec(memory_space=pltpu.SMEM)
    whole = pl.BlockSpec(own.shape, lambda i: (0, 0, 0))
    return pl.pallas_call(
        both_kernel,
        grid=(tokens // rows,),
        out_shape=(
            jax.ShapeDtypeStruct((tokens, outs), bf16),
            jax.ShapeDtypeStruct((tokens, features), bf16),
        ),
        in_specs=[
            smem,
            smem,
            pl.BlockSpec((rows, features), lambda i: (i, 0)),
            pl.BlockSpec((rows, 1), lambda i: (i, 0)),
            pl.BlockSpec((1, features), lambda i: (0, 0)),
            pl.BlockSpec((rows, outs), lambda i: (i, 0)),
            pl.BlockSpec((1, rows), lambda i: (0, i)),
            whole,
            whole,
        ],
        out_specs=(
            pl.BlockSpec((rows, outs), lambda i: (i, 0)),
            pl.BlockSpec((rows, features), lambda i: (i, 0)),
        ),
        scratch_shapes=[
            pltpu.VMEM((features // 16, 16, outs), bf16),
            pltpu.VMEM((rows, features), f32),
        ],
        compiler_params=pltpu.CompilerParams(vmem_limit_bytes=48 * 2**20),
        cost_estimate=pl.CostEstimate(
            flops=4 * tokens * features * outs, bytes_accessed=13 * 2**20, transcendentals=0
        ),
        name="values_and_input_grad",
    )(me, jnp.asarray(OFFSET_OF), hidden, inv, gain, cot, ids, own, other)


def shards(
    hidden_states, norm_gain, master_weight, first_moment, second_moment, token_ids, out_cotangent
):
    tokens_all = hidden_states.shape[0] * DEVICES
    grad_scale = 1.0 / math.sqrt(tokens_all)
    features = hidden_states.shape[1]
    rows, outs = master_weight.shape
    index = lax.axis_index("grp") * lax.axis_size("loc") + lax.axis_index("loc")
    me = index.astype(jnp.int32).reshape(1)
    gain_row = norm_gain.reshape(1, features)
    ids_row = token_ids.reshape(1, -1)

    weight_bf = master_weight.astype(bf16)
    held = weight_bf.reshape(1, rows, outs)
    for mask in STEPS[:0:-1]:
        held = jnp.concatenate([held, exchange(held, mask)], axis=0)
    other = exchange(held, CORE)

    inv, keep, send = local_grad(me, hidden_states, gain_row, out_cotangent, ids_row)
    total = keep + exchange(send, CORE).astype(f32)
    for mask in STEPS[1:]:
        half = total.shape[0] // 2
        leave = total[half:]
        if half > 2:
            leave = leave.astype(bf16)
        total = total[:half] + exchange(leave, mask).astype(f32)
    summed = total.reshape(rows, outs)

    value_heads, input_grad = values_and_input_grad(
        me, hidden_states, inv, gain_row, out_cotangent, ids_row, held, other
    )

    weight_grad = summed * grad_scale
    new_first = beta_one * first_moment + (1.0 - beta_one) * weight_grad
    new_second = beta_two * second_moment + (1.0 - beta_two) * weight_grad * weight_grad
    first_bias = 1.0 - beta_one**STEP
    second_bias = 1.0 - beta_two**STEP
    update = new_first / first_bias / (jnp.sqrt(new_second / second_bias) + adam_epsilon)
    new_master = master_weight - learning_rate * (update + weight_decay * master_weight)

    gain_rows = jnp.sum(weight_grad * weight_bf.astype(f32), axis=1).reshape(1, rows)
    gain_all = lax.all_to_all(
        jnp.broadcast_to(gain_rows, (DEVICES, rows)), AXES, split_axis=0, concat_axis=0, tiled=True
    )
    gain_grad = gain_all.reshape(features) / norm_gain
    return (value_heads, input_grad, gain_grad, new_master, new_first, new_second)


def solution(mesh):
    in_specs = (
        P(("grp", "loc"), None),
        P(),
        P(("grp", "loc"), None),
        P(("grp", "loc"), None),
        P(("grp", "loc"), None),
        P(("grp", "loc")),
        P(("grp", "loc"), None),
    )
    out_specs = (
        P(("grp", "loc"), None),
        P(("grp", "loc"), None),
        P(),
        P(("grp", "loc"), None),
        P(("grp", "loc"), None),
        P(("grp", "loc"), None),
    )
    return jax.shard_map(shards, mesh=mesh, in_specs=in_specs, out_specs=out_specs, check_vma=False)
```

```python
import functools
import math

import jax
import jax.numpy as jnp
import numpy as np
from jax import lax
from jax.experimental import pallas as pl
from jax.experimental.pallas import tpu as pltpu
from jax.sharding import PartitionSpec as P

RESERVED = 256
STEP = 10

norm_epsilon = 1e-05
beta_one = 0.9
beta_two = 0.95
adam_epsilon = 1e-08
learning_rate = 0.001
weight_decay = 0.1

bf16 = jnp.bfloat16
f32 = jnp.float32
AXES = ("grp", "loc")
DEVICES = 256

CORE = 1
X1, X3, Y1, Y3 = 2, 6, 32, 96
Z1, Z2, Z6 = 128, 8, 24
A1, A3, B1, B3 = (X1, Y1), (X3, Y3), (Y1, X1), (Y3, X3)
A13, B13 = (X1 ^ X3, Y1 ^ Y3), (Y1 ^ Y3, X1 ^ X3)
HALVES = 2
PARTS = 2
CHUNKS = 4
STEPS = ((CORE, A1, A3, B1, B3, Z6, Z2, Z1), (CORE, A3, A1, B1, B3, Z6, Z2, Z1))


def mask_of(mask, core):
    return mask[core] if isinstance(mask, tuple) else mask


def offsets(steps, core):
    own, other = ([0], [0])
    for mask in steps[:0:-1]:
        own = own + [o ^ mask_of(mask, core) for o in own]
        other = other + [o ^ mask_of(mask, 1 - core) for o in other]
    return own + [o ^ CORE for o in other]


OFFSET_OF = np.array([[offsets(s, 0), offsets(s, 1)] for s in STEPS], np.int32)
POSITION_OF = np.argsort(OFFSET_OF, axis=2).astype(np.int32)
TABLE = np.concatenate([POSITION_OF.reshape(-1), OFFSET_OF.reshape(-1)])


def position(table_ref, which, core, offset):
    return table_ref[(2 * which + core) * DEVICES + offset]


def offset_at(table_ref, which, core, place):
    return table_ref[(2 * HALVES + 2 * which + core) * DEVICES + place]


def exchange(x, mask):
    pairs = [(i, i ^ mask_of(mask, i & 1)) for i in range(DEVICES)]
    return lax.ppermute(x, AXES, pairs)


def column(row):
    return jnp.transpose(jnp.broadcast_to(row, (8, row.shape[1])))[:, :1]


def params(mib):
    return pltpu.CompilerParams(vmem_limit_bytes=mib * 2**20)


VMEM = pl.BlockSpec(memory_space=pltpu.VMEM)
SMEM = pl.BlockSpec(memory_space=pltpu.SMEM)


def grad_kernel(me_ref, table_hbm, h_hbm, gain_hbm, cot_hbm, ids_hbm, inv_ref, masked_ref, keep0_ref, send0_ref, keep1_ref, send1_ref, table_ref, h_ref, gain_ref, cot_ref, ids_ref, normed_ref, blk_ref, sems):
    tokens, features = h_ref.shape
    rows = tokens // CHUNKS
    me = me_ref[0]
    core = jnp.bitwise_and(me, 1)
    small = [
        pltpu.make_async_copy(source, target, sems.at[CHUNKS + i])
        for i, (source, target) in enumerate(
            ((ids_hbm, ids_ref), (gain_hbm, gain_ref), (cot_hbm, cot_ref), (table_hbm, table_ref))
        )
    ]
    copies = []
    for c in range(CHUNKS):
        at = pl.ds(c * rows, rows)
        copies.append(pltpu.make_async_copy(h_hbm.at[at], h_ref.at[at], sems.at[c]))
    small[0].start()
    small[1].start()
    copies[0].start()
    small[2].start()
    small[3].start()
    for copy in copies[1:]:
        copy.start()
    for copy in small:
        copy.wait()
    live = column(ids_ref[...]) >= RESERVED
    masked = jnp.where(live, cot_ref[...], jnp.zeros_like(cot_ref))
    masked_ref[...] = masked
    for c, copy in enumerate(copies):
        copy.wait()
        of = slice(c * rows, c * rows + rows)
        total = jnp.zeros((rows, 128), f32)
        for j in range(features // 128):
            x = h_ref[of, 128 * j : 128 * j + 128].astype(f32)
            total = total + x * x
        mean = jnp.sum(total, axis=1, keepdims=True) * (1.0 / features)
        inv = lax.rsqrt(mean + norm_epsilon)
        inv_ref[of, :] = inv
        for j in range(features // 512):
            at = slice(512 * j, 512 * j + 512)
            normed = ((h_ref[of, at].astype(f32) * inv) * gain_ref[:, at]).astype(bf16)
            normed_ref[at, of] = jnp.transpose(normed)
    width = blk_ref.shape[1] * blk_ref.shape[2]
    wide = keep0_ref.shape[2]
    for j in range(features // width):
        slot = j % 2
        part = jnp.dot(
            normed_ref[j * width : (j + 1) * width, :], masked, preferred_element_type=f32
        )
        blk_ref[slot] = part.reshape(blk_ref.shape[1:])
        first = j * (width // 16)
        for i in range(width // 32):
            own = 2 * i + core
            away = 2 * i + (1 - core)
            for which, keep_ref, send_ref in ((0, keep0_ref, send0_ref), (1, keep1_ref, send1_ref)):
                at = slice(which * wide, which * wide + wide)
                p = position(table_ref, which, core, jnp.bitwise_xor(first + own, me))
                q = position(table_ref, which, core, jnp.bitwise_xor(first + away, me))
                keep_ref[p] = blk_ref[slot, own, :, at]
                send_ref[q - DEVICES // 2] = blk_ref[slot, away, :, at].astype(bf16)


def local_grad(me, table, hidden, gain, cot, ids):
    tokens, features = hidden.shape
    outs = cot.shape[1]
    half = features // 32
    keep = jax.ShapeDtypeStruct((half, 16, outs // HALVES), f32)
    send = jax.ShapeDtypeStruct((half, 16, outs // HALVES), bf16)
    return pl.pallas_call(
        grad_kernel,
        out_shape=(
            jax.ShapeDtypeStruct((tokens, 1), f32),
            jax.ShapeDtypeStruct((tokens, outs), bf16),
            keep,
            send,
            keep,
            send,
        ),
        in_specs=[SMEM] + [pl.BlockSpec(memory_space=pltpu.HBM)] * 5,
        out_specs=(VMEM,) * 6,
        scratch_shapes=[
            pltpu.SMEM(table.shape, jnp.int32),
            pltpu.VMEM((tokens, features), bf16),
            pltpu.VMEM((1, features), f32),
            pltpu.VMEM((tokens, outs), bf16),
            pltpu.VMEM((1, tokens), jnp.int32),
            pltpu.VMEM((features, tokens), bf16),
            pltpu.VMEM((2, 32, 16, outs), f32),
            pltpu.SemaphoreType.DMA((CHUNKS + 4,)),
        ],
        compiler_params=params(46),
        cost_estimate=pl.CostEstimate(
            flops=2 * tokens * features * outs, bytes_accessed=12 * 2**20, transcendentals=0
        ),
        name="local_grad",
    )(me, table, hidden, gain, cot, ids)


def split_kernel(keep_ref, got_ref, kept_ref, leave_ref):
    half = kept_ref.shape[0]
    kept_ref[...] = keep_ref[:half] + got_ref[:half].astype(f32)
    leave_ref[...] = (keep_ref[half:] + got_ref[half:].astype(f32)).astype(bf16)


def split(keep, got):
    blocks, rows, outs = keep.shape
    return pl.pallas_call(
        split_kernel,
        out_shape=(
            jax.ShapeDtypeStruct((blocks // 2, rows, outs), f32),
            jax.ShapeDtypeStruct((blocks // 2, rows, outs), bf16),
        ),
        in_specs=[VMEM, VMEM],
        out_specs=(VMEM, VMEM),
        compiler_params=params(6),
        name="split",
    )(keep, got)


def merge_kernel(me_ref, table_ref, keep0_ref, got0_ref, keep1_ref, got1_ref, w_ref, keep_ref, send_ref, gain_ref):
    blocks = w_ref.shape[0]
    wide = keep0_ref.shape[2]
    me = me_ref[0]
    core = jnp.bitwise_and(me, 1)
    lane = lax.broadcasted_iota(jnp.int32, (16, 128), 1)
    gain = jnp.zeros((16, 128), f32)
    for p in range(blocks):
        left = keep0_ref[p] + got0_ref[p].astype(f32)
        right = keep1_ref[p] + got1_ref[p].astype(f32)
        w = w_ref[p].astype(f32)
        prod = left * w[:, :wide] + right * w[:, wide:]
        row = jnp.sum(prod, axis=1, keepdims=True)
        at = jnp.bitwise_xor(offset_at(table_ref, 0, core, p), me) // 2
        gain = gain + jnp.where(lane == at, row, 0.0)
        if p < blocks // 2:
            keep_ref[p, :, :wide] = left
            keep_ref[p, :, wide:] = right
        else:
            send_ref[p - blocks // 2, :, :wide] = left.astype(bf16)
            send_ref[p - blocks // 2, :, wide:] = right.astype(bf16)
    gain_ref[...] = gain


def merge(me, table, keep0, got0, keep1, got1, w):
    blocks, rows, outs = w.shape
    return pl.pallas_call(
        merge_kernel,
        out_shape=(
            jax.ShapeDtypeStruct((blocks // 2, rows, outs), f32),
            jax.ShapeDtypeStruct((blocks // 2, rows, outs), bf16),
            jax.ShapeDtypeStruct((rows, 128), f32),
        ),
        in_specs=[SMEM, SMEM] + [VMEM] * 5,
        out_specs=(VMEM, VMEM, VMEM),
        compiler_params=params(8),
        name="merge",
    )(me, table, keep0, got0, keep1, got1, w)


def place_kernel(me_ref, table_ref, own0_ref, other0_ref, own1_ref, other1_ref, w_ref):
    me = me_ref[0]
    core = jnp.bitwise_and(me, 1)
    half = DEVICES // 2
    wide = own0_ref.shape[2]

    def place(p, carry):
        for which, own_ref, other_ref in ((0, own0_ref, other0_ref), (1, own1_ref, other1_ref)):
            columns = slice(which * wide, which * wide + wide)
            near = jnp.bitwise_xor(offset_at(table_ref, which, core, p), me)
            far = jnp.bitwise_xor(offset_at(table_ref, which, core, p + half), me)
            w_ref[near, :, columns] = own_ref[p]
            w_ref[far, :, columns] = other_ref[p]
        return carry

    lax.fori_loop(0, half, place, 0, unroll=8)


def whole_weight(me, table, pieces):
    blocks, rows, wide = pieces[0].shape
    return pl.pallas_call(
        place_kernel,
        out_shape=jax.ShapeDtypeStruct((2 * blocks, rows, HALVES * wide), bf16),
        in_specs=[SMEM, SMEM] + [VMEM] * 4,
        out_specs=VMEM,
        compiler_params=params(10),
        name="whole_weight",
    )(me, table, *pieces)


def both_kernel(h_ref, inv_ref, gain_ref, masked_ref, w_ref, *refs):
    values_ref, grad_ref, wt_ref = refs[-3:]
    tokens, features = h_ref.shape
    width = 512
    inv = inv_ref[...]
    masked = masked_ref[...]
    values = jnp.zeros(values_ref.shape, f32)
    inner = jnp.zeros((tokens, 128), f32)
    for j in range(features // width):
        at = slice(j * width, j * width + width)
        w = w_ref[j * (width // 16) : (j + 1) * (width // 16)].reshape(width, w_ref.shape[2])
        gain = gain_ref[:, at]
        scaled = h_ref[:, at].astype(f32) * inv
        values = values + jnp.dot((scaled * gain).astype(bf16), w, preferred_element_type=f32)
        back = lax.dot_general(masked, w, (((1,), (1,)), ((), ())), preferred_element_type=f32)
        weighted = back * gain
        wt_ref[:, at] = weighted
        prod = weighted * scaled
        for k in range(width // 128):
            inner = inner + prod[:, 128 * k : 128 * k + 128]
    values_ref[...] = values.astype(bf16)
    mean = jnp.sum(inner, axis=1, keepdims=True) * (1.0 / features)
    for j in range(features // width):
        at = slice(j * width, j * width + width)
        scaled = h_ref[:, at].astype(f32) * inv
        grad_ref[:, at] = ((wt_ref[:, at] - scaled * mean) * inv).astype(bf16)


def values_and_input_grad(hidden, inv, gain, masked, weight, part, made):
    tokens, features = hidden.shape
    outs = masked.shape[1]
    rows = tokens // PARTS
    left = pl.BlockSpec(memory_space=pl.ANY)
    return pl.pallas_call(
        both_kernel,
        grid=(1,),
        out_shape=(
            jax.ShapeDtypeStruct((tokens, outs), bf16),
            jax.ShapeDtypeStruct((tokens, features), bf16),
        ),
        in_specs=[
            pl.BlockSpec((rows, features), lambda i: (i + part, 0)),
            pl.BlockSpec((rows, 1), lambda i: (i + part, 0)),
            pl.BlockSpec((1, features), lambda i: (0, 0)),
            pl.BlockSpec((rows, outs), lambda i: (i + part, 0)),
            VMEM,
        ]
        + [left] * len(made),
        out_specs=(
            pl.BlockSpec((rows, outs), lambda i: (i + part, 0)),
            pl.BlockSpec((rows, features), lambda i: (i + part, 0)),
        ),
        scratch_shapes=[pltpu.VMEM((rows, features), f32)],
        input_output_aliases={5 + i: i for i in range(len(made))},
        compiler_params=params(16),
        cost_estimate=pl.CostEstimate(
            flops=4 * rows * features * outs, bytes_accessed=6 * 2**20, transcendentals=0
        ),
        name="values_and_input_grad",
    )(hidden, inv, gain, masked, weight, *made)


together = lax.optimization_barrier


def grow(held, got):
    return jnp.concatenate([held, got], axis=0)


def unpack(got):
    blocks, last = got[:-1].astype(f32), got[-1].astype(f32)
    return blocks, (last[:, :128] + last[:, 128:256]) + last[:, 256:384]


def pack(blocks, gain):
    high = gain.astype(bf16)
    rest = gain - high.astype(f32)
    middle = rest.astype(bf16)
    low = (rest - middle.astype(f32)).astype(bf16)
    last = jnp.concatenate([high, middle, low, jnp.zeros_like(low)], axis=1)
    return jnp.concatenate([blocks.astype(bf16), last[None]], axis=0)


def unpack_wide(got):
    last = got[-1]
    return got[:-1], jnp.concatenate([last[:, :128], last[:, 128:256]], axis=0)


def pack_wide(blocks, gain):
    rows = gain.shape[0] // 2
    last = jnp.concatenate([gain[:rows], gain[rows:]], axis=1)
    last = jnp.pad(last, ((0, 0), (0, blocks.shape[2] - last.shape[1])))
    return jnp.concatenate([blocks, last[None]], axis=0)


def shards(
    hidden_states, norm_gain, master_weight, first_moment, second_moment, token_ids, out_cotangent
):
    tokens_all = hidden_states.shape[0] * DEVICES
    grad_scale = 1.0 / math.sqrt(tokens_all)
    features = hidden_states.shape[1]
    rows, outs = master_weight.shape
    wide = outs // HALVES
    index = lax.axis_index("grp") * lax.axis_size("loc") + lax.axis_index("loc")
    me = index.astype(jnp.int32).reshape(1)
    table = jnp.asarray(TABLE)
    gain_row = norm_gain.reshape(1, features)
    ids_row = token_ids.reshape(1, -1)

    held = master_weight.astype(bf16).reshape(1, rows, outs)
    got = exchange(held, Z1)
    inv, masked, keep0, send0, keep1, send1 = local_grad(
        me, table, hidden_states, gain_row, out_cotangent, ids_row
    )
    held, got, send0, send1 = together((held, got, send0, send1))

    held = grow(held, got)
    swap0 = exchange(send0, CORE)
    swap1 = exchange(send1, CORE)
    got = exchange(held, Z2)
    got, swap0, swap1 = together((got, swap0, swap1))

    held = grow(held, got)
    keep0, send0 = split(keep0, swap0)
    keep1, send1 = split(keep1, swap1)
    held, send0, send1 = together((held, send0, send1))
    got0, got1 = exchange(send0, A1), exchange(send1, A3)
    held = grow(held, exchange(held, Z6))
    got = exchange(held, B3)
    got, got0, got1 = together((got, got0, got1))

    held = grow(held, got)
    keep0, send0 = split(keep0, got0)
    keep1, send1 = split(keep1, got1)
    held, send0, send1 = together((held, send0, send1))
    got = exchange(held, B1)
    got0, got1 = exchange(send0, A3), exchange(send1, A1)
    held = grow(held, got)
    part0, part1 = held[:, :, :wide], held[:, :, wide:]
    more0, more1 = exchange(part0, A3), exchange(part1, A1)

    part0, part1 = grow(part0, more0), grow(part1, more1)
    keep, send, gain = merge(me, table, keep0, got0, keep1, got1, held)
    got = exchange(send, B1)
    more0, more1 = exchange(part0, A1), exchange(part1, A3)
    near, next_to, across = exchange(gain, A1), exchange(gain, A3), exchange(gain, A13)
    gain = (gain + near) + (next_to + across)

    part0, part1 = grow(part0, more0), grow(part1, more1)
    more0, more1 = exchange(part0, CORE), exchange(part1, CORE)
    total = keep + got.astype(f32)
    half = total.shape[0] // 2
    keep, got = total[:half], exchange(pack(total[half:], gain), B3)
    near, across = exchange(gain, B1), exchange(gain, B13)

    weight = whole_weight(me, table, (part0, more0, part1, more1))

    def finish(part, made=()):
        return values_and_input_grad(hidden_states, inv, gain_row, masked, weight, part, made)

    blocks, other = unpack(got)
    total, gain = keep + blocks, (gain + near) + (other + across)
    half = total.shape[0] // 2
    keep, got = total[:half], exchange(pack(total[half:], gain), Z6)
    near, across = exchange(gain, CORE), exchange(gain, CORE ^ Z6)
    made = finish(0)
    got, made = together((got, made))

    blocks, other = unpack(got)
    total, mine, other = keep + blocks, gain + other, near + across
    core = jnp.bitwise_and(index, 1)
    gain = jnp.concatenate(
        [jnp.where(core == 0, mine, other), jnp.where(core == 0, other, mine)], axis=0
    )
    half = total.shape[0] // 2
    keep, got = total[:half], exchange(pack_wide(total[half:], gain), Z2)
    made = finish(1, made)
    got, made = together((got, made))
    value_heads, input_grad = made

    blocks, other = unpack_wide(got)
    total, gain = keep + blocks, gain + other
    half = total.shape[0] // 2
    got = exchange(pack_wide(total[half:], gain), Z1)
    blocks, other = unpack_wide(got)
    total, gain = total[:half] + blocks, gain + other
    summed = total.reshape(rows, outs)

    gain_grad = jnp.transpose(gain).reshape(features) * grad_scale / norm_gain

    weight_grad = summed * grad_scale
    new_first = beta_one * first_moment + (1.0 - beta_one) * weight_grad
    new_second = beta_two * second_moment + (1.0 - beta_two) * weight_grad * weight_grad
    first_bias = 1.0 - beta_one**STEP
    second_bias = 1.0 - beta_two**STEP
    update = new_first / first_bias / (jnp.sqrt(new_second / second_bias) + adam_epsilon)
    new_master = master_weight - learning_rate * (update + weight_decay * master_weight)
    return (value_heads, input_grad, gain_grad, new_master, new_first, new_second)


def solution(mesh):
    in_specs = (
        P(("grp", "loc"), None),
        P(),
        P(("grp", "loc"), None),
        P(("grp", "loc"), None),
        P(("grp", "loc"), None),
        P(("grp", "loc")),
        P(("grp", "loc"), None),
    )
    out_specs = (
        P(("grp", "loc"), None),
        P(("grp", "loc"), None),
        P(),
        P(("grp", "loc"), None),
        P(("grp", "loc"), None),
        P(("grp", "loc"), None),
    )
    return jax.shard_map(shards, mesh=mesh, in_specs=in_specs, out_specs=out_specs, check_vma=False)
```
